768 devices in a mesh: seq: 48 (over z, x), tp: 16 (over y, core).
Axes of the slice: x: 4, y: 8, z: 12, core: 2. Of those that a mesh axis runs over, the one named last changes fastest.
Arguments:
- hidden: bfloat16 [49152, 3584], P('seq', 'tp'), may hold values from -6 to 6
- grad_out: bfloat16 [49152, 3584], P('seq', 'tp'), may hold values from -24 to 24
- router_w: float32 [3584], replicated, may hold values from -0.09375 to 0.09375
- norm_gain: bfloat16 [3584], replicated, may hold values from 0.099609375 to 1.8984375
- gate_w: bfloat16 [3584, 7168], P(None, 'tp'), may hold values from -0.09375 to 0.09375
- up_w: bfloat16 [3584, 7168], P(None, 'tp'), may hold values from -0.09375 to 0.09375
- down_w: bfloat16 [7168, 3584], P('tp'), may hold values from -0.0625 to 0.0625
- counts: int32 [48], P('seq'), may hold values from 1 to 384, 6144 in all
- order: int32 [48, 1024], P('seq'), may hold values from 0 to 1023, each once within a row
Outputs:
- unit_scores: float32 [3, 7168], P(None, 'tp')
- router_score: float32 [3584], P('tp')
The draws below stay inside these ranges and needn't reach their ends.
Inputs may be any that keep to these rules, and one draw needn't show every extreme that they name: The counts sum to 6144; the largest is exactly 384. `order`: each row is a permutation of the shard's local token indices.
All inputs are finite; a program needn't handle non-finite values. No bound on the sum of `counts` on one device may be relied on, other than what follows from the above.
Results may differ from the reference program's by a relative error of at most 0.0043.
Values may be sent and summed in bfloat16 or wider, within the bound.
A program may use at most 64 MiB of HBM per device.

```python
import math
import jax
import jax.numpy as jnp
import numpy as np
from jax import lax

D = 3584
FF = 7168
TOK_DEV = 1024
SHARDS = 48
TOKENS = 49152
CAP = 128
SLOTS = 384
SELECTED = 6144


def block_levels(key, dims, shards, least, top_value):
    def one(position, shards_of):
        steps = jax.random.uniform(jax.random.fold_in(jax.random.fold_in(key, 6), position), (shards_of,), jnp.float32, least / len(shards), top_value / len(shards))
        return jnp.repeat(jnp.exp(steps), dims[position] // shards_of).reshape((-1,) + (1,) * (len(dims) - position - 1))

    gain = one(*shards[0])
    for cut in shards[1:]:
        gain = gain * one(*cut)
    return gain


def length_profile(count, total, limit, skew):
    weights = [(1 << 20) // math.isqrt(grade ** skew) + 1 for grade in range(2, count + 1)]
    spare, holding = total - limit - (count - 1), [1] * (count - 1)
    while spare > 0:
        candidates = [i for i in range(count - 1) if holding[i] < limit]
        pool, remaining = sum([weights[i] for i in candidates]), spare
        for i in candidates:
            addition = min(limit - holding[i], max(1, remaining * weights[i] // pool), spare)
            holding[i] = holding[i] + addition
            spare = spare - addition
    return np.array([limit] + holding)


def ragged(stream_key, number_of, total, reach, skew):
    if number_of == 2:
        one = jax.random.randint(stream_key, (), max(1, total - reach), min(reach, total - 1) + 1)
        return jnp.stack([one, total - one])
    tallies = jnp.asarray(length_profile(number_of, total, reach, skew), jnp.int32)
    pairs = (number_of - 1) // 2
    donor, receiver = tallies[1:1 + 2 * pairs:2], tallies[2:2 + 2 * pairs:2]
    margin = jnp.minimum(donor - 1, reach - receiver)
    passed = jax.random.randint(jax.random.fold_in(stream_key, 1), (pairs,), 0, 1 << 20) % (margin + 1)
    tallies = tallies.at[1:1 + 2 * pairs:2].set(donor - passed).at[2:2 + 2 * pairs:2].set(receiver + passed)
    return tallies[jax.random.permutation(jax.random.fold_in(stream_key, 2), number_of)]


def centred(own_key, shape, width, limit, shards=(), held_as=jnp.bfloat16):
    gain = block_levels(own_key, shape, shards, -0.22, 0.18) if shards else 1.0
    array = jax.random.normal(own_key, shape, jnp.float32) * width * gain
    return jnp.minimum(jnp.maximum(array, -limit), limit).astype(held_as)


def setup_inputs(seed: int = 0) -> dict:
    arg_keys = jax.random.split(jax.random.key(seed), 10)
    return {
        "hidden": centred(arg_keys[0], (TOKENS, D), 1.0, 6.0, ((0, 48), (1, 16))),
        "grad_out": centred(arg_keys[1], (TOKENS, D), 4.0, 24.0, ((0, 48), (1, 16))),
        "router_w": centred(arg_keys[2], (D,), D ** -0.5, 0.09375, (), jnp.float32),
        "norm_gain": jnp.clip(1.0 + 0.18 * jax.random.normal(arg_keys[3], (D,), jnp.float32), 0.099609375, 1.8984375).astype(jnp.bfloat16),
        "gate_w": centred(arg_keys[4], (D, FF), D ** -0.5, 0.09375, ((1, 16),)),
        "up_w": centred(arg_keys[5], (D, FF), D ** -0.5, 0.09375, ((1, 16),)),
        "down_w": centred(arg_keys[6], (FF, D), FF ** -0.5, 0.0625, ((0, 16),)),
        "counts": ragged(arg_keys[7], SHARDS, SELECTED, SLOTS, 2).astype(jnp.int32),
        "order": jax.vmap(lambda own: jax.random.permutation(own, TOK_DEV))(jax.random.split(arg_keys[8], SHARDS)).reshape((SHARDS, TOK_DEV)).astype(jnp.int32),
    }


epsilon = 1e-06

def gelu_pair(gate_proj):
    activation, pullback = jax.vjp(lambda inputs: jax.nn.gelu(inputs, approximate=True), gate_proj)
    slope = pullback(jnp.ones_like(gate_proj))[0]
    return (activation, slope)

def reference(hidden, grad_out, router_w, norm_gain, gate_w, up_w, down_w, counts, order):
    positions = jnp.arange(SLOTS, dtype=jnp.int32)
    live_rows = positions[None, :] < counts[:, None]
    global_index = (jnp.arange(SHARDS, dtype=jnp.int32)[:, None] * TOK_DEV + order[:, :SLOTS]).reshape(-1)
    flat_live = live_rows.reshape(-1)
    running = jnp.cumsum(flat_live.astype(jnp.int32)) - 1
    target_row = jnp.where(flat_live, running, SELECTED).astype(jnp.int32)
    row_index = jnp.zeros((SELECTED + 1,), jnp.int32).at[target_row].set(global_index)[:SELECTED]
    groups = row_index.reshape(SHARDS, CAP)
    gain_f32 = norm_gain.astype(jnp.float32)

    def accumulate(totals, indices):
        unit_sum, router_sum = totals
        feature_rows = hidden[indices]
        cotangent_rows = grad_out[indices]
        feature_f32 = feature_rows.astype(jnp.float32)
        inverse_rms = lax.rsqrt(lax.optimization_barrier(jnp.sum(feature_f32 * feature_f32, axis=1)) / D + epsilon)
        logits = lax.optimization_barrier(jnp.sum(feature_f32 * router_w, axis=1))
        scaled_rows = (feature_f32 * gain_f32).astype(jnp.bfloat16)
        gate_proj = jnp.dot(scaled_rows, gate_w, preferred_element_type=jnp.float32) * inverse_rms[:, None]
        up_proj = jnp.dot(scaled_rows, up_w, preferred_element_type=jnp.float32) * inverse_rms[:, None]
        back_proj = jnp.dot(cotangent_rows, down_w.T, preferred_element_type=jnp.float32)
        router_prob = jax.nn.sigmoid(logits)
        activation, slope = gelu_pair(gate_proj)
        hidden_units = activation * up_proj
        grad_hidden = router_prob[:, None] * back_proj
        unit_terms = jnp.stack([lax.optimization_barrier(jnp.sum(gate_proj * grad_hidden * up_proj * slope, axis=0)), lax.optimization_barrier(jnp.sum(up_proj * grad_hidden * activation, axis=0)), lax.optimization_barrier(jnp.sum(hidden_units * grad_hidden, axis=0))])
        router_coef = router_prob * (1.0 - router_prob) * lax.optimization_barrier(jnp.sum(hidden_units * back_proj, axis=1))
        router_terms = lax.optimization_barrier(jnp.sum(router_coef[:, None] * feature_f32, axis=0))
        return ((unit_sum + unit_terms, router_sum + router_terms), None)
    start_totals = (jnp.zeros((3, FF), jnp.float32), jnp.zeros((D,), jnp.float32))
    totals, _ = lax.scan(accumulate, start_totals, groups)
    factor = float(SELECTED) ** (-0.5)
    return (totals[0] * factor, router_w * totals[1] * factor)
```

```python
import functools

import jax
import jax.numpy as jnp
from jax import lax
from jax.experimental import pallas as pl
from jax.experimental.pallas import tpu as pltpu
from jax.sharding import PartitionSpec as P

MESH = pl.DeviceIdType.MESH
LANES = 128
CORES = 2
X_CHIPS = 4
EPSILON = 1e-06
ROOT = 0.7978845608028654
CUBIC = 0.044715


def column(row):
    return jnp.transpose(jnp.broadcast_to(row, (LANES, LANES)))


def kernel(
    sizes,
    hidden_hbm, grad_hbm, router_hbm, gain_hbm, gate_hbm, up_hbm, down_hbm, counts_ref, order_hbm,
    unit_ref, score_ref,
    hidden_v, grad_v, gate_v, up_v, down_v, router_v, gain_v, order_v, held, gain_col, router_col,
    gate_sum, up_sum, back_sum, unit_sum, dots, unit_x, unit_z, score_x, score_z,
    load_sem, near_sem, ring_send, ring_recv, dot_send, dot_recv, ux_send, ux_recv, uz_send, uz_recv,
    sx_send, sx_recv, sz_send, sz_recv,
):
    xs, zs, ys, chunks, factor = sizes
    tp = ys * CORES
    width = hidden_v.shape[0]
    tokens = hidden_v.shape[1]
    features = width * tp
    seq_me = lax.axis_index("seq")
    tp_me = lax.axis_index("tp")
    x_me, z_me = lax.rem(seq_me, xs), seq_me // xs
    y_me, core = tp_me // CORES, lax.rem(tp_me, CORES)
    sibling = y_me * CORES + (1 - core)

    def block_at(distance, of_core):
        return lax.rem(y_me + distance + ys, ys) * CORES + of_core

    right, left = block_at(1, core), block_at(-1, core)

    loads = [
        pltpu.make_async_copy(source, target, load_sem.at[i])
        for i, (source, target) in enumerate(
            [
                (order_hbm, order_v), (hidden_hbm, hidden_v), (grad_hbm, grad_v),
                (router_hbm, router_v), (gain_hbm, gain_v), (gate_hbm, gate_v), (up_hbm, up_v), (down_hbm, down_v),
            ]
        )
    ]
    for load in loads:
        load.start()

    barrier = pltpu.get_barrier_semaphore()
    along_x = lambda i: z_me * xs + lax.rem(i + xs, xs)
    along_z = lambda i: lax.rem(i + zs, zs) * xs + x_me
    beside_x = [along_x(x_me + i) for i in ((1, -1) if xs > 2 else (1,) if xs > 1 else ())]
    beside_z = [along_z(z_me + i) for i in ((1, -1) if zs > 2 else (1,) if zs > 1 else ())]
    beside_y = [right, left] if ys > 2 else [right]
    for peer in beside_y + [sibling]:
        pl.semaphore_signal(barrier, inc=1, device_id={"tp": peer}, device_id_type=MESH)
    for peer in beside_x + beside_z:
        pl.semaphore_signal(barrier, inc=1, device_id={"seq": peer}, device_id_type=MESH)

    rounds = max(zs // 2, xs // 2) - 1

    def relay(i):
        if not 0 <= i < rounds:
            return
        peers = (beside_x if i + 1 < xs // 2 else []) + (beside_z if i + 1 < zs // 2 else [])
        if i > 0:
            relay_wait(i - 1)
        for peer in peers:
            pl.semaphore_signal(near_sem.at[i], inc=1, device_id={"seq": peer}, device_id_type=MESH)

    def relay_wait(i):
        peers = (beside_x if i + 1 < xs // 2 else []) + (beside_z if i + 1 < zs // 2 else [])
        if peers:
            pl.semaphore_wait(near_sem.at[i], len(peers))

    token = lax.broadcasted_iota(jnp.int32, (tokens, LANES), 0)
    slot = lax.broadcasted_iota(jnp.int32, (1, LANES), 1)
    loads[0].wait()
    count = counts_ref[0]

    def select(chunk):
        wanted = order_v[:, chunk * LANES : (chunk + 1) * LANES]
        wanted = jnp.where(slot + chunk * LANES < count, wanted, -1)
        chosen = jnp.where(token == wanted, 1.0, 0.0).astype(jnp.bfloat16)
        if chunk == 0:
            loads[1].wait()
        rows = jnp.dot(hidden_v[...], chosen, preferred_element_type=jnp.float32)
        held[chunk, 0, tp_me] = rows.astype(jnp.bfloat16)
        if chunk == 0:
            loads[2].wait()
        rows = jnp.dot(grad_v[...], chosen, preferred_element_type=jnp.float32)
        held[chunk, 1, tp_me] = rows.astype(jnp.bfloat16)

    select(0)
    pl.semaphore_wait(barrier, len(beside_y) + 1 + len(beside_x) + len(beside_z))

    sent = []

    def pass_on(chunk, array, block, way):
        target = (right, left, sibling)[way]
        copy = pltpu.make_async_remote_copy(
            src_ref=held.at[chunk, array, block],
            dst_ref=held.at[chunk, array, block],
            send_sem=ring_send.at[chunk, array, block, way],
            recv_sem=ring_recv.at[chunk, array, block],
            device_id={"tp": target},
            device_id_type=MESH,
        )
        copy.start()
        sent.append(copy)

    def arrive(chunk, array, block):
        pltpu.make_async_copy(
            held.at[chunk, array, block], held.at[chunk, array, block], ring_recv.at[chunk, array, block]
        ).wait()

    half = ys // 2

    def open_ring(chunk):
        for way in range(3):
            for array in range(2):
                pass_on(chunk, array, tp_me, way)

    def ring_step(chunk, distance):
        last = distance == half
        for array in range(2):
            for way in range(2):
                if last and array != way:
                    continue
                block = block_at(-distance if way == 0 else distance, core)
                arrive(chunk, array, block)
                if distance + 1 < half or (distance + 1 == half and array == way):
                    pass_on(chunk, array, block, way)
                pass_on(chunk, array, block, 2)

    def sibling_step(chunk, distance):
        for array in range(2):
            for way in range(2):
                if distance == 0 and way == 1 or distance == half and way != array:
                    continue
                arrive(chunk, array, block_at(-distance if way == 0 else distance, 1 - core))

    groups = ys // 2
    first = y_me // 2
    lean = 2 * lax.rem(y_me, 2) - 1
    group_order = [first] if groups == 1 else [first, first + lean, first - lean, first + 2]
    group_after = [1, 2, 3, 4]
    if groups == 2:
        group_order, group_after = [first, first + 1], [1, 2]
    if groups == 1:
        group_after = [1]
    depth = features // groups

    def multiply(chunk, place):
        group = lax.rem(group_order[place] + groups, groups)
        at = pl.ds(pl.multiple_of(group * depth, LANES), depth)
        pieces = pl.ds(group * (tp // groups), tp // groups)
        values = held[chunk, 0, pieces].reshape(depth, LANES).astype(jnp.float32)
        scaled = (values * gain_col[at, :]).astype(jnp.bfloat16)
        squares = jnp.sum(values * values, axis=0, keepdims=True)
        logit = jnp.sum(values * router_col[at, :], axis=0, keepdims=True)
        cotangent = held[chunk, 1, pieces].reshape(depth, LANES)
        gate = jnp.dot(gate_v[:, at], scaled, preferred_element_type=jnp.float32)
        up = jnp.dot(up_v[:, at], scaled, preferred_element_type=jnp.float32)
        back = jnp.dot(down_v[:, at], cotangent, preferred_element_type=jnp.float32)
        if place == 0:
            gate_sum[chunk] = gate
            up_sum[chunk] = up
            back_sum[chunk] = back
        else:
            gate_sum[chunk] += gate
            up_sum[chunk] += up
            back_sum[chunk] += back
        return squares, logit

    def share_dots(chunk):
        copies = []
        for step in range(1, tp):
            copy = pltpu.make_async_remote_copy(
                src_ref=dots.at[chunk, tp_me],
                dst_ref=dots.at[chunk, tp_me],
                send_sem=dot_send.at[chunk, step],
                recv_sem=dot_recv.at[chunk, tp_me],
                device_id={"tp": lax.rem(tp_me + step, tp)},
                device_id_type=MESH,
            )
            copy.start()
            sent.append(copy)

    def await_dots(chunk):
        for step in range(1, tp):
            peer = lax.rem(tp_me + step, tp)
            pltpu.make_async_copy(dots.at[chunk, peer], dots.at[chunk, peer], dot_recv.at[chunk, peer]).wait()

    def finish(chunk, squares, logit):
        inverse = lax.rsqrt(squares / features + EPSILON)
        prob = 1.0 / (1.0 + jnp.exp(-logit))
        gate = gate_sum[chunk] * inverse
        up = up_sum[chunk] * inverse
        back = back_sum[chunk]
        square = gate * gate
        bend = jnp.tanh(ROOT * gate * (1.0 + CUBIC * square))
        plus = 0.5 * (1.0 + bend)
        slope = plus + 0.5 * gate * (1.0 - bend * bend) * (ROOT * (1.0 + (3.0 * CUBIC) * square))
        act = gate * plus
        h_back = act * up * back
        dots[chunk, tp_me] = jnp.sum(h_back, axis=0, keepdims=True)
        share_dots(chunk)
        term = gate * up * slope * back * prob
        if chunk == 0:
            unit_sum[0] = term
            unit_sum[1] = h_back * prob
        else:
            unit_sum[0] += term
            unit_sum[1] += h_back * prob
        return prob

    open_ring(0)
    for chunk in range(1, chunks):
        select(chunk)
        open_ring(chunk)
    relay(0)
    loads[3].wait()
    loads[4].wait()
    gain = gain_v[...].astype(jnp.float32)
    for i in range(features // LANES):
        at = slice(i * LANES, (i + 1) * LANES)
        gain_col[at, :] = column(gain[at].reshape(1, LANES))
        router_col[at, :] = column(router_v[at].reshape(1, LANES))
    for load in loads[5:]:
        load.wait()

    probs = []
    totals = [None] * chunks
    for chunk in range(chunks):
        sibling_step(chunk, 0)
    done = 0
    for distance in range(1, half + 1):
        for chunk in range(chunks):
            ring_step(chunk, distance)
        relay(distance)
        ready = done < len(group_after) and group_after[done] <= distance
        for chunk in range(chunks):
            sibling_step(chunk, distance)
            if ready:
                more = multiply(chunk, done)
                totals[chunk] = more if done == 0 else (totals[chunk][0] + more[0], totals[chunk][1] + more[1])
            if distance == half:
                probs.append(finish(chunk, *totals[chunk]))
        done += int(ready)

    def share(buffer, send, recv, mine, count_of, peer_of):
        for step in range(1, count_of):
            copy = pltpu.make_async_remote_copy(
                src_ref=buffer.at[mine],
                dst_ref=buffer.at[mine],
                send_sem=send.at[step],
                recv_sem=recv.at[mine],
                device_id={"seq": peer_of(lax.rem(mine + step, count_of))},
                device_id_type=MESH,
            )
            copy.start()
            sent.append(copy)

    def collect(buffer, recv, mine, count_of):
        for step in range(1, count_of):
            peer = lax.rem(mine + step, count_of)
            pltpu.make_async_copy(buffer.at[peer], buffer.at[peer], recv.at[peer]).wait()
        total = buffer[0]
        for i in range(1, count_of):
            total = total + buffer[i]
        return total

    for i in range(half + 1, rounds):
        relay(i)
    if rounds > 0:
        relay_wait(rounds - 1)

    for i in range(2):
        unit_x[x_me, i : i + 1, :] = jnp.sum(jnp.transpose(unit_sum[i]), axis=0, keepdims=True)
    share(unit_x, ux_send, ux_recv, x_me, xs, along_x)

    weighted = None
    for chunk in range(chunks):
        await_dots(chunk)
        total = dots[chunk, 0]
        for i in range(1, tp):
            total = total + dots[chunk, i]
        coef = probs[chunk] * (1.0 - probs[chunk]) * total
        more = held[chunk, 0, tp_me].astype(jnp.float32) * coef
        weighted = more if weighted is None else weighted + more
    weighted = weighted * router_col[pl.ds(pl.multiple_of(tp_me * width, 8), width), :]
    score_x[x_me] = jnp.sum(jnp.transpose(weighted), axis=0, keepdims=True)
    share(score_x, sx_send, sx_recv, x_me, xs, along_x)

    unit_z[z_me] = collect(unit_x, ux_recv, x_me, xs)
    share(unit_z, uz_send, uz_recv, z_me, zs, along_z)
    score_z[z_me] = collect(score_x, sx_recv, x_me, xs)
    share(score_z, sz_send, sz_recv, z_me, zs, along_z)

    unit = collect(unit_z, uz_recv, z_me, zs) * factor
    unit_ref[0:2, :] = unit
    unit_ref[2:3, :] = unit[1:2, :]
    score_ref[...] = collect(score_z, sz_recv, z_me, zs) * factor
    for copy in sent:
        copy.wait_send()


def body(sizes, hidden, grad_out, router_w, norm_gain, gate_w, up_w, down_w, counts, order):
    xs, zs, ys, chunks, factor = sizes
    tp = ys * CORES
    tokens, width = hidden.shape
    features, units = gate_w.shape
    dma = pltpu.SemaphoreType.DMA
    f32, bf16 = jnp.float32, jnp.bfloat16
    anywhere = pl.BlockSpec(memory_space=pl.ANY)
    in_vmem = pl.BlockSpec(memory_space=pltpu.VMEM)
    unit, score = pl.pallas_call(
        functools.partial(kernel, sizes),
        out_shape=(jax.ShapeDtypeStruct((3, units), f32), jax.ShapeDtypeStruct((1, width), f32)),
        in_specs=[
            anywhere, anywhere, anywhere, anywhere, anywhere, anywhere, anywhere,
            pl.BlockSpec(memory_space=pltpu.SMEM), anywhere,
        ],
        out_specs=(in_vmem, in_vmem),
        scratch_shapes=[
            pltpu.VMEM((width, tokens), bf16),
            pltpu.VMEM((width, tokens), bf16),
            pltpu.VMEM((units, features), bf16),
            pltpu.VMEM((units, features), bf16),
            pltpu.VMEM((units, features), bf16),
            pltpu.VMEM((features,), f32),
            pltpu.VMEM((features,), bf16),
            pltpu.VMEM((1, order.shape[1]), jnp.int32),
            pltpu.VMEM((chunks, 2, tp, width, LANES), bf16),
            pltpu.VMEM((features, LANES), f32),
            pltpu.VMEM((features, LANES), f32),
            pltpu.VMEM((chunks, units, LANES), f32),
            pltpu.VMEM((chunks, units, LANES), f32),
            pltpu.VMEM((chunks, units, LANES), f32),
            pltpu.VMEM((2, units, LANES), f32),
            pltpu.VMEM((chunks, tp, 1, LANES), f32),
            pltpu.VMEM((xs, 2, units), f32),
            pltpu.VMEM((zs, 2, units), f32),
            pltpu.VMEM((xs, 1, width), f32),
            pltpu.VMEM((zs, 1, width), f32),
            dma((8,)),
            pltpu.SemaphoreType.REGULAR((8,)),
            dma((chunks, 2, tp, 3)),
            dma((chunks, 2, tp)),
            dma((chunks, tp)),
            dma((chunks, tp)),
            dma((xs,)),
            dma((xs,)),
            dma((zs,)),
            dma((zs,)),
            dma((xs,)),
            dma((xs,)),
            dma((zs,)),
            dma((zs,)),
        ],
        compiler_params=pltpu.CompilerParams(
            collective_id=0, has_side_effects=True, vmem_limit_bytes=62 * 1024 * 1024
        ),
    )(
        hidden.T,
        grad_out.T,
        router_w,
        norm_gain,
        gate_w.T,
        up_w.T,
        down_w,
        counts,
        order,
    )
    return unit, score.reshape(width)


def solution(mesh):
    seq, tp = mesh.shape["seq"], mesh.shape["tp"]
    xs = X_CHIPS if seq % X_CHIPS == 0 else 1
    chunks = 3
    sizes = (xs, seq // xs, tp // CORES, chunks, float(LANES * seq) ** -0.5)
    in_specs = (
        P("seq", "tp"),
        P("seq", "tp"),
        P(),
        P(),
        P(None, "tp"),
        P(None, "tp"),
        P("tp", None),
        P("seq"),
        P("seq", None),
    )
    return jax.shard_map(
        functools.partial(body, sizes),
        mesh=mesh,
        in_specs=in_specs,
        out_specs=(P(None, "tp"), P("tp")),
        check_vma=False,
    )
```

```python
import functools

import jax
import jax.numpy as jnp
from jax import lax
from jax.experimental import pallas as pl
from jax.experimental.pallas import tpu as pltpu
from jax.sharding import PartitionSpec as P

MESH = pl.DeviceIdType.MESH
LANES = 128
CORES = 2
X_CHIPS = 4
EPSILON = 1e-06
ROOT = 0.7978845608028654
CUBIC = 0.044715


def column(row):
    return jnp.transpose(jnp.broadcast_to(row, (LANES, LANES)))


def kernel(
    sizes,
    hidden_hbm, grad_hbm, router_hbm, gain_hbm, gate_hbm, up_hbm, down_hbm, counts_hbm, order_hbm,
    unit_ref, score_ref,
    hidden_v, grad_v, gate_v, up_v, down_v, router_v, gain_v, order_v, count_v, held, gain_col, router_col,
    gate_sum, up_sum, back_sum, unit_sum, dots, unit_x, unit_z, score_all,
    load_sem, near_sem, ring_send, ring_recv, dot_send, dot_recv, ux_send, ux_recv, uz_send, uz_recv,
    score_send, score_recv,
):
    xs, zs, ys, chunks, factor = sizes
    tp = ys * CORES
    width = hidden_v.shape[0]
    tokens = hidden_v.shape[1]
    features = width * tp
    seq_me = lax.axis_index("seq")
    tp_me = lax.axis_index("tp")
    x_me, z_me = lax.rem(seq_me, xs), seq_me // xs
    y_me, core = tp_me // CORES, lax.rem(tp_me, CORES)
    sibling = y_me * CORES + (1 - core)

    def block_at(distance, of_core):
        return lax.rem(y_me + distance + ys, ys) * CORES + of_core

    right, left = block_at(1, core), block_at(-1, core)

    loads = [
        pltpu.make_async_copy(source, target, load_sem.at[i])
        for i, (source, target) in enumerate(
            [
                (order_hbm, order_v), (counts_hbm, count_v), (hidden_hbm, hidden_v), (grad_hbm, grad_v),
                (router_hbm, router_v), (gain_hbm, gain_v), (gate_hbm, gate_v), (up_hbm, up_v), (down_hbm, down_v),
            ]
        )
    ]
    for load in loads[:4]:
        load.start()

    barrier = pltpu.get_barrier_semaphore()
    along_x = lambda i: z_me * xs + lax.rem(i + xs, xs)
    along_z = lambda i: lax.rem(i + zs, zs) * xs + x_me
    beside_x = [along_x(x_me + i) for i in ((1, -1) if xs > 2 else (1,) if xs > 1 else ())]
    beside_z = [along_z(z_me + i) for i in ((1, -1) if zs > 2 else (1,) if zs > 1 else ())]
    beside_y = [right, left] if ys > 2 else [right]
    for peer in beside_y + [sibling]:
        pl.semaphore_signal(barrier, inc=1, device_id={"tp": peer}, device_id_type=MESH)
    for peer in beside_x + beside_z:
        pl.semaphore_signal(barrier, inc=1, device_id={"seq": peer}, device_id_type=MESH)

    rounds = zs // 2 + xs // 2 - 1
    relayed = []

    def relay():
        i = len(relayed)
        if i > rounds:
            return
        relayed.append(i)
        if i > 0:
            pl.semaphore_wait(near_sem.at[i - 1], len(beside_x + beside_z))
        if i < rounds:
            for peer in beside_x + beside_z:
                pl.semaphore_signal(near_sem.at[i], inc=1, device_id={"seq": peer}, device_id_type=MESH)

    token = lax.broadcasted_iota(jnp.int32, (tokens, LANES), 0)
    slot = lax.broadcasted_iota(jnp.int32, (1, LANES), 1)
    loads[0].wait()
    loads[1].wait()
    count = count_v[0]

    def choose(chunk):
        wanted = order_v[:, chunk * LANES : (chunk + 1) * LANES]
        wanted = jnp.where(slot + chunk * LANES < count, wanted, -1)
        return jnp.where(token == wanted, 1.0, 0.0).astype(jnp.bfloat16)

    def pick(chunk, array, chosen):
        rows = jnp.dot((hidden_v, grad_v)[array][...], chosen, preferred_element_type=jnp.float32)
        held[chunk, array, tp_me] = rows.astype(jnp.bfloat16)

    ring_sent = [0] * chunks

    def pass_on(chunk, array, block, way):
        target = (right, left, sibling)[way]
        copy = pltpu.make_async_remote_copy(
            src_ref=held.at[chunk, array, block],
            dst_ref=held.at[chunk, array, block],
            send_sem=ring_send.at[chunk],
            recv_sem=ring_recv.at[chunk, array, block],
            device_id={"tp": target},
            device_id_type=MESH,
        )
        copy.start()
        ring_sent[chunk] += 1

    def await_bytes(view, semaphore):
        pltpu.make_async_copy(view, view, semaphore).wait()

    def arrive(chunk, array, block):
        pltpu.make_async_copy(
            held.at[chunk, array, block], held.at[chunk, array, block], ring_recv.at[chunk, array, block]
        ).wait()

    half = ys // 2

    def open_ring(chunk):
        chosen = choose(chunk)
        for array in range(2):
            if chunk == 0:
                loads[2 + array].wait()
            pick(chunk, array, chosen)
            if chunk == 0 and array == 0:
                pl.semaphore_wait(barrier, len(beside_y) + 1 + len(beside_x) + len(beside_z))
            for way in range(2):
                if half > 1 or way == array:
                    pass_on(chunk, array, tp_me, way)

    def ring_step(chunk, distance):
        last = distance == half
        for array in range(2):
            for way in range(2):
                if last and array != way:
                    continue
                block = block_at(-distance if way == 0 else distance, core)
                arrive(chunk, array, block)
                if distance + 1 < half or (distance + 1 == half and array == way):
                    pass_on(chunk, array, block, way)
                pass_on(chunk, array, block, 2)

    def sibling_step(chunk, distance):
        for array in range(2):
            for way in range(2):
                if distance == 0 and way == 1 or distance == half and way != array:
                    continue
                arrive(chunk, array, block_at(-distance if way == 0 else distance, 1 - core))

    groups = ys // 2
    first = y_me // 2
    lean = 2 * lax.rem(y_me, 2) - 1
    group_order = [first] if groups == 1 else [first, first + lean, first - lean, first + 2]
    group_after = [1, 2, 3, 4]
    if groups == 2:
        group_order, group_after = [first, first + 1], [1, 2]
    if groups == 1:
        group_after = [1]
    depth = features // groups

    def multiply(chunk, place):
        group = lax.rem(group_order[place] + groups, groups)
        at = pl.ds(pl.multiple_of(group * depth, LANES), depth)
        pieces = pl.ds(group * (tp // groups), tp // groups)
        values = held[chunk, 0, pieces].reshape(depth, LANES).astype(jnp.float32)
        scaled = (values * gain_col[at, :]).astype(jnp.bfloat16)
        squares = jnp.sum(values * values, axis=0, keepdims=True)
        logit = jnp.sum(values * router_col[at, :], axis=0, keepdims=True)
        cotangent = held[chunk, 1, pieces].reshape(depth, LANES)
        gate = jnp.dot(gate_v[:, at], scaled, preferred_element_type=jnp.float32)
        up = jnp.dot(up_v[:, at], scaled, preferred_element_type=jnp.float32)
        back = jnp.dot(down_v[:, at], cotangent, preferred_element_type=jnp.float32)
        if place == 0:
            gate_sum[chunk] = gate
            up_sum[chunk] = up
            back_sum[chunk] = back
        else:
            gate_sum[chunk] += gate
            up_sum[chunk] += up
            back_sum[chunk] += back
        return squares, logit

    def far_first(count_of, gap):
        return sorted(range(1, count_of), key=lambda step: -min(step // gap, (count_of - step) // gap))

    def share_dots():
        for step in far_first(tp, CORES):
            copy = pltpu.make_async_remote_copy(
                src_ref=dots.at[tp_me],
                dst_ref=dots.at[tp_me],
                send_sem=dot_send.at[0],
                recv_sem=dot_recv.at[0],
                device_id={"tp": lax.rem(tp_me + step, tp)},
                device_id_type=MESH,
            )
            copy.start()

    def finish(chunk, squares, logit):
        inverse = lax.rsqrt(squares / features + EPSILON)
        prob = 1.0 / (1.0 + jnp.exp(-logit))
        gate = gate_sum[chunk] * inverse
        up = up_sum[chunk] * inverse
        back = back_sum[chunk]
        square = gate * gate
        bend = jnp.tanh(ROOT * gate * (1.0 + CUBIC * square))
        plus = 0.5 * (1.0 + bend)
        slope = plus + 0.5 * gate * (1.0 - bend * bend) * (ROOT * (1.0 + (3.0 * CUBIC) * square))
        act = gate * plus
        h_back = act * up * back
        dots[tp_me, chunk : chunk + 1, :] = jnp.sum(h_back, axis=0, keepdims=True)
        term = gate * up * slope * back * prob
        if chunk == 0:
            unit_sum[0] = term
            unit_sum[1] = h_back * prob
        else:
            unit_sum[0] += term
            unit_sum[1] += h_back * prob
        return prob

    for chunk in range(chunks):
        open_ring(chunk)
        if chunk == 0:
            relay()
            for load in loads[4:]:
                load.start()
    relay()
    for chunk in range(chunks):
        for array in range(2):
            pass_on(chunk, array, tp_me, 2)
    loads[4].wait()
    loads[5].wait()
    gain = gain_v[...].astype(jnp.float32)
    for i in range(features // LANES):
        at = slice(i * LANES, (i + 1) * LANES)
        gain_col[at, :] = column(gain[at].reshape(1, LANES))
        router_col[at, :] = column(router_v[at].reshape(1, LANES))
    for load in loads[6:]:
        load.wait()

    probs = [None] * chunks
    totals = [None] * chunks

    def compute(chunk, place):
        sibling_step(chunk, group_after[place])
        more = multiply(chunk, place)
        totals[chunk] = more if place == 0 else (totals[chunk][0] + more[0], totals[chunk][1] + more[1])
        if place == len(group_after) - 1:
            probs[chunk] = finish(chunk, *totals[chunk])

    for chunk in range(chunks):
        sibling_step(chunk, 0)
    waiting = []
    for distance in range(1, half + 1):
        for chunk in range(chunks):
            ring_step(chunk, distance)
            if waiting:
                compute(*waiting.pop(0))
            if distance in group_after:
                waiting.append((chunk, group_after.index(distance)))
            relay()
    for item in waiting:
        compute(*item)
    share_dots()

    def share(buffer, send, recv, mine, count_of, peer_of):
        for step in far_first(count_of, 1):
            copy = pltpu.make_async_remote_copy(
                src_ref=buffer.at[mine],
                dst_ref=buffer.at[mine],
                send_sem=send.at[0],
                recv_sem=recv.at[0],
                device_id={"seq": peer_of(lax.rem(mine + step, count_of))},
                device_id_type=MESH,
            )
            copy.start()

    def sent(buffer, send, count_of):
        if count_of > 1:
            await_bytes(buffer.at[pl.ds(0, count_of - 1)], send.at[0])

    def collect(buffer, recv, count_of):
        if count_of > 1:
            await_bytes(buffer.at[pl.ds(0, count_of - 1)], recv.at[0])
        total = buffer[0]
        for i in range(1, count_of):
            total = total + buffer[i]
        return total

    while len(relayed) <= rounds:
        relay()

    for i in range(2):
        unit_x[x_me, i : i + 1, :] = jnp.sum(jnp.transpose(unit_sum[i]), axis=0, keepdims=True)
    share(unit_x, ux_send, ux_recv, x_me, xs, along_x)
    for chunk in range(chunks):
        assert ring_sent[chunk] == 2 * (tp - 1)
        await_bytes(held.at[chunk, :, pl.ds(0, tp - 1)], ring_send.at[chunk])

    await_bytes(dots.at[pl.ds(0, tp - 1)], dot_recv.at[0])
    total = dots[0]
    for i in range(1, tp):
        total = total + dots[i]
    weighted = None
    for chunk in range(chunks):
        coef = probs[chunk] * (1.0 - probs[chunk]) * total[chunk : chunk + 1, :]
        more = held[chunk, 0, tp_me].astype(jnp.float32) * coef
        weighted = more if weighted is None else weighted + more
    weighted = weighted * router_col[pl.ds(pl.multiple_of(tp_me * width, 8), width), :]
    score_all[seq_me] = jnp.sum(jnp.transpose(weighted), axis=0, keepdims=True)
    ways = [(i, j) for i in range(zs) for j in range(xs) if i + j]
    for i, j in sorted(ways, key=lambda way: -min(way[0], zs - way[0]) - min(way[1], xs - way[1])):
        copy = pltpu.make_async_remote_copy(
            src_ref=score_all.at[seq_me],
            dst_ref=score_all.at[seq_me],
            send_sem=score_send.at[0],
            recv_sem=score_recv.at[0],
            device_id={"seq": lax.rem(z_me + i, zs) * xs + lax.rem(x_me + j, xs)},
            device_id_type=MESH,
        )
        copy.start()

    unit_z[z_me] = collect(unit_x, ux_recv, xs)
    share(unit_z, uz_send, uz_recv, z_me, zs, along_z)
    await_bytes(dots.at[pl.ds(0, tp - 1)], dot_send.at[0])
    sent(unit_x, ux_send, xs)

    unit = collect(unit_z, uz_recv, zs) * factor
    unit_ref[0:2, :] = unit
    unit_ref[2:3, :] = unit[1:2, :]
    sent(unit_z, uz_send, zs)
    score_ref[...] = collect(score_all, score_recv, xs * zs) * factor
    sent(score_all, score_send, xs * zs)


def body(sizes, hidden, grad_out, router_w, norm_gain, gate_w, up_w, down_w, counts, order):
    xs, zs, ys, chunks, factor = sizes
    tp = ys * CORES
    tokens, width = hidden.shape
    features, units = gate_w.shape
    dma = pltpu.SemaphoreType.DMA
    f32, bf16 = jnp.float32, jnp.bfloat16
    in_hbm = pl.BlockSpec(memory_space=pl.ANY)
    in_vmem = pl.BlockSpec(memory_space=pltpu.VMEM)
    unit, score = pl.pallas_call(
        functools.partial(kernel, sizes),
        out_shape=(jax.ShapeDtypeStruct((3, units), f32), jax.ShapeDtypeStruct((1, width), f32)),
        in_specs=[
            in_hbm, in_hbm, in_hbm, in_hbm, in_hbm, in_hbm, in_hbm, in_hbm, in_hbm,
        ],
        out_specs=(in_vmem, in_vmem),
        scratch_shapes=[
            pltpu.VMEM((width, tokens), bf16),
            pltpu.VMEM((width, tokens), bf16),
            pltpu.VMEM((units, features), bf16),
            pltpu.VMEM((units, features), bf16),
            pltpu.VMEM((units, features), bf16),
            pltpu.VMEM((features,), f32),
            pltpu.VMEM((features,), bf16),
            pltpu.VMEM((1, order.shape[1]), jnp.int32),
            pltpu.SMEM((1,), jnp.int32),
            pltpu.VMEM((chunks, 2, tp, width, LANES), bf16),
            pltpu.VMEM((features, LANES), f32),
            pltpu.VMEM((features, LANES), f32),
            pltpu.VMEM((chunks, units, LANES), f32),
            pltpu.VMEM((chunks, units, LANES), f32),
            pltpu.VMEM((chunks, units, LANES), f32),
            pltpu.VMEM((2, units, LANES), f32),
            pltpu.VMEM((tp, chunks, LANES), f32),
            pltpu.VMEM((xs, 2, units), f32),
            pltpu.VMEM((zs, 2, units), f32),
            pltpu.VMEM((xs * zs, 1, width), f32),
            dma((9,)),
            pltpu.SemaphoreType.REGULAR((8,)),
            dma((chunks,)),
            dma((chunks, 2, tp)),
            dma((1,)),
            dma((1,)),
            dma((1,)),
            dma((1,)),
            dma((1,)),
            dma((1,)),
            dma((1,)),
            dma((1,)),
        ],
        compiler_params=pltpu.CompilerParams(
            collective_id=0, has_side_effects=True, vmem_limit_bytes=62 * 1024 * 1024
        ),
    )(
        hidden.T,
        grad_out.T,
        router_w,
        norm_gain,
        gate_w.T,
        up_w.T,
        down_w,
        counts,
        order,
    )
    return unit, score.reshape(width)


def solution(mesh):
    seq, tp = mesh.shape["seq"], mesh.shape["tp"]
    xs = X_CHIPS if seq % X_CHIPS == 0 else 1
    chunks = 3
    sizes = (xs, seq // xs, tp // CORES, chunks, float(LANES * seq) ** -0.5)
    in_specs = (
        P("seq", "tp"),
        P("seq", "tp"),
        P(),
        P(),
        P(None, "tp"),
        P(None, "tp"),
        P("tp", None),
        P("seq"),
        P("seq", None),
    )
    return jax.shard_map(
        functools.partial(body, sizes),
        mesh=mesh,
        in_specs=in_specs,
        out_specs=(P(None, "tp"), P("tp")),
        check_vma=False,
    )
```

```python
import functools

import jax
import jax.numpy as jnp
from jax import lax
from jax.experimental import pallas as pl
from jax.experimental.pallas import tpu as pltpu
from jax.sharding import PartitionSpec as P

MESH = pl.DeviceIdType.MESH
LANES = 128
CORES = 2
X_CHIPS = 4
EPSILON = 1e-06
ROOT = 0.7978845608028654
CUBIC = 0.044715


def column(row):
    return jnp.transpose(jnp.broadcast_to(row, (LANES, LANES)))


def kernel(
    sizes,
    hidden_hbm, grad_hbm, router_hbm, gain_hbm, gate_hbm, up_hbm, down_hbm, counts_hbm, order_hbm,
    unit_ref, score_ref,
    hidden_v, grad_v, gate_v, up_v, down_v, router_v, gain_v, order_v, count_v, held, gain_col, router_col,
    gate_sum, up_sum, back_sum, unit_sum, dots, unit_x, unit_z, score_all,
    load_sem, near_sem, ring_send, ring_recv, dot_send, dot_recv, ux_send, ux_recv, uz_send, uz_recv,
    score_send, score_recv,
):
    xs, zs, ys, chunks, factor = sizes
    tp = ys * CORES
    width = hidden_v.shape[0]
    tokens = hidden_v.shape[1]
    features = width * tp
    seq_me = lax.axis_index("seq")
    tp_me = lax.axis_index("tp")
    x_me, z_me = lax.rem(seq_me, xs), seq_me // xs
    y_me, core = tp_me // CORES, lax.rem(tp_me, CORES)
    sibling = y_me * CORES + (1 - core)

    def block_at(distance, of_core):
        return lax.rem(y_me + distance + ys, ys) * CORES + of_core

    right, left = block_at(1, core), block_at(-1, core)

    loads = [
        pltpu.make_async_copy(source, target, load_sem.at[i])
        for i, (source, target) in enumerate(
            [
                (order_hbm, order_v), (counts_hbm, count_v), (hidden_hbm, hidden_v), (grad_hbm, grad_v),
                (router_hbm, router_v), (gain_hbm, gain_v), (gate_hbm, gate_v), (up_hbm, up_v), (down_hbm, down_v),
            ]
        )
    ]
    for load in loads[:4]:
        load.start()

    barrier = pltpu.get_barrier_semaphore()
    along_x = lambda i: z_me * xs + lax.rem(i + xs, xs)
    along_z = lambda i: lax.rem(i + zs, zs) * xs + x_me
    beside_x = [along_x(x_me + i) for i in ((1, -1) if xs > 2 else (1,) if xs > 1 else ())]
    beside_z = [along_z(z_me + i) for i in ((1, -1) if zs > 2 else (1,) if zs > 1 else ())]
    beside_y = [right, left] if ys > 2 else [right]
    for peer in beside_y + [sibling]:
        pl.semaphore_signal(barrier, inc=1, device_id={"tp": peer}, device_id_type=MESH)
    for peer in beside_x + beside_z:
        pl.semaphore_signal(barrier, inc=1, device_id={"seq": peer}, device_id_type=MESH)

    rounds = zs // 2 + xs // 2 - 1
    relayed = []

    def relay():
        i = len(relayed)
        if i > rounds:
            return
        relayed.append(i)
        if i > 0:
            pl.semaphore_wait(near_sem.at[i - 1], len(beside_x + beside_z))
        if i < rounds:
            for peer in beside_x + beside_z:
                pl.semaphore_signal(near_sem.at[i], inc=1, device_id={"seq": peer}, device_id_type=MESH)

    token = lax.broadcasted_iota(jnp.int32, (tokens, LANES), 0)
    slot = lax.broadcasted_iota(jnp.int32, (1, LANES), 1)
    loads[0].wait()
    loads[1].wait()
    count = count_v[0]

    def choose(chunk):
        wanted = order_v[:, chunk * LANES : (chunk + 1) * LANES]
        wanted = jnp.where(slot + chunk * LANES < count, wanted, -1)
        return jnp.where(token == wanted, 1.0, 0.0).astype(jnp.bfloat16)

    def pick(chunk, array, chosen):
        rows = jnp.dot((hidden_v, grad_v)[array][...], chosen, preferred_element_type=jnp.float32)
        held[chunk, array, tp_me] = rows.astype(jnp.bfloat16)

    ring_sent = [0] * chunks

    def pass_on(chunk, array, block, way):
        target = (right, left, sibling)[way]
        copy = pltpu.make_async_remote_copy(
            src_ref=held.at[chunk, array, block],
            dst_ref=held.at[chunk, array, block],
            send_sem=ring_send.at[chunk],
            recv_sem=ring_recv.at[chunk, array, block],
            device_id={"tp": target},
            device_id_type=MESH,
        )
        copy.start()
        ring_sent[chunk] += 1

    def await_bytes(view, semaphore):
        pltpu.make_async_copy(view, view, semaphore).wait()

    def arrive(chunk, array, block):
        pltpu.make_async_copy(
            held.at[chunk, array, block], held.at[chunk, array, block], ring_recv.at[chunk, array, block]
        ).wait()

    half = ys // 2

    def open_ring(chunk):
        chosen = choose(chunk)
        for array in range(2):
            if chunk == 0:
                loads[2 + array].wait()
            pick(chunk, array, chosen)
            if chunk == 0 and array == 0:
                pl.semaphore_wait(barrier, len(beside_y) + 1 + len(beside_x) + len(beside_z))
            for way in range(2):
                if half > 1 or way == array:
                    pass_on(chunk, array, tp_me, way)

    def ring_step(chunk, distance):
        last = distance == half
        for array in range(2):
            for way in range(2):
                if last and array != way:
                    continue
                block = block_at(-distance if way == 0 else distance, core)
                arrive(chunk, array, block)
                if distance + 1 < half or (distance + 1 == half and array == way):
                    pass_on(chunk, array, block, way)
                pass_on(chunk, array, block, 2)

    def sibling_step(chunk, distance):
        for array in range(2):
            for way in range(2):
                if distance == 0 and way == 1 or distance == half and way != array:
                    continue
                arrive(chunk, array, block_at(-distance if way == 0 else distance, 1 - core))

    groups = ys // 2
    first = y_me // 2
    lean = 2 * lax.rem(y_me, 2) - 1
    group_order = [first] if groups == 1 else [first, first + lean, first - lean, first + 2]
    group_after = [1, 2, 3, 4]
    if groups == 2:
        group_order, group_after = [first, first + 1], [1, 2]
    if groups == 1:
        group_after = [1]
    depth = features // groups

    def multiply(chunk, place):
        group = lax.rem(group_order[place] + groups, groups)
        at = pl.ds(pl.multiple_of(group * depth, LANES), depth)
        pieces = pl.ds(group * (tp // groups), tp // groups)
        values = held[chunk, 0, pieces].reshape(depth, LANES).astype(jnp.float32)
        scaled = (values * gain_col[at, :]).astype(jnp.bfloat16)
        squares = jnp.sum(values * values, axis=0, keepdims=True)
        logit = jnp.sum(values * router_col[at, :], axis=0, keepdims=True)
        cotangent = held[chunk, 1, pieces].reshape(depth, LANES)
        gate = jnp.dot(gate_v[:, at], scaled, preferred_element_type=jnp.float32)
        up = jnp.dot(up_v[:, at], scaled, preferred_element_type=jnp.float32)
        back = jnp.dot(down_v[:, at], cotangent, preferred_element_type=jnp.float32)
        if place == 0:
            gate_sum[chunk] = gate
            up_sum[chunk] = up
            back_sum[chunk] = back
        else:
            gate_sum[chunk] += gate
            up_sum[chunk] += up
            back_sum[chunk] += back
        return squares, logit

    def far_first(count_of, gap):
        return sorted(range(1, count_of), key=lambda step: -min(step // gap, (count_of - step) // gap))

    def share_dots():
        for step in far_first(tp, CORES):
            copy = pltpu.make_async_remote_copy(
                src_ref=dots.at[tp_me],
                dst_ref=dots.at[tp_me],
                send_sem=dot_send.at[0],
                recv_sem=dot_recv.at[0],
                device_id={"tp": lax.rem(tp_me + step, tp)},
                device_id_type=MESH,
            )
            copy.start()

    def finish(chunk, squares, logit):
        inverse = lax.rsqrt(squares / features + EPSILON)
        prob = 1.0 / (1.0 + jnp.exp(-logit))
        gate = gate_sum[chunk] * inverse
        up = up_sum[chunk] * inverse
        back = back_sum[chunk]
        square = gate * gate
        bend = jnp.tanh(ROOT * gate * (1.0 + CUBIC * square))
        plus = 0.5 * (1.0 + bend)
        slope = plus + 0.5 * gate * (1.0 - bend * bend) * (ROOT * (1.0 + (3.0 * CUBIC) * square))
        act = gate * plus
        h_back = act * up * back
        dots[tp_me, chunk : chunk + 1, :] = jnp.sum(h_back, axis=0, keepdims=True)
        term = gate * up * slope * back * prob
        if chunk == 0:
            unit_sum[0] = term
            unit_sum[1] = h_back * prob
        else:
            unit_sum[0] += term
            unit_sum[1] += h_back * prob
        return prob

    for chunk in range(chunks):
        open_ring(chunk)
        if chunk == 0:
            relay()
            for load in loads[4:]:
                load.start()
    relay()
    for chunk in range(chunks):
        for array in range(2):
            pass_on(chunk, array, tp_me, 2)
    loads[4].wait()
    loads[5].wait()
    gain = gain_v[...].astype(jnp.float32)
    for i in range(features // LANES):
        at = slice(i * LANES, (i + 1) * LANES)
        gain_col[at, :] = column(gain[at].reshape(1, LANES))
        router_col[at, :] = column(router_v[at].reshape(1, LANES))
    for load in loads[6:]:
        load.wait()

    probs = [None] * chunks
    totals = [None] * chunks

    def compute(chunk, place):
        sibling_step(chunk, group_after[place])
        more = multiply(chunk, place)
        totals[chunk] = more if place == 0 else (totals[chunk][0] + more[0], totals[chunk][1] + more[1])
        if place == len(group_after) - 1:
            probs[chunk] = finish(chunk, *totals[chunk])

    for chunk in range(chunks):
        sibling_step(chunk, 0)
    waiting = []
    for distance in range(1, half + 1):
        for chunk in range(chunks):
            ring_step(chunk, distance)
            if waiting:
                compute(*waiting.pop(0))
            if distance in group_after:
                waiting.append((chunk, group_after.index(distance)))
            relay()
    for item in waiting:
        compute(*item)
    share_dots()

    def share(buffer, send, recv, mine, count_of, peer_of):
        for step in far_first(count_of, 1):
            copy = pltpu.make_async_remote_copy(
                src_ref=buffer.at[mine],
                dst_ref=buffer.at[mine],
                send_sem=send.at[0],
                recv_sem=recv.at[0],
                device_id={"seq": peer_of(lax.rem(mine + step, count_of))},
                device_id_type=MESH,
            )
            copy.start()

    def sent(buffer, send, count_of):
        if count_of > 1:
            await_bytes(buffer.at[pl.ds(0, count_of - 1)], send.at[0])

    def collect(buffer, recv, count_of):
        if count_of > 1:
            await_bytes(buffer.at[pl.ds(0, count_of - 1)], recv.at[0])
        total = buffer[0]
        for i in range(1, count_of):
            total = total + buffer[i]
        return total

    while len(relayed) <= rounds:
        relay()

    for i in range(2):
        unit_x[x_me, i : i + 1, :] = jnp.sum(jnp.transpose(unit_sum[i]), axis=0, keepdims=True)
    share(unit_x, ux_send, ux_recv, x_me, xs, along_x)
    for chunk in range(chunks):
        assert ring_sent[chunk] == 2 * (tp - 1)
        await_bytes(held.at[chunk, :, pl.ds(0, tp - 1)], ring_send.at[chunk])

    await_bytes(dots.at[pl.ds(0, tp - 1)], dot_recv.at[0])
    total = dots[0]
    for i in range(1, tp):
        total = total + dots[i]
    weighted = None
    for chunk in range(chunks):
        coef = probs[chunk] * (1.0 - probs[chunk]) * total[chunk : chunk + 1, :]
        more = held[chunk, 0, tp_me].astype(jnp.float32) * coef
        weighted = more if weighted is None else weighted + more
    weighted = weighted * router_col[pl.ds(pl.multiple_of(tp_me * width, 8), width), :]
    score_all[seq_me] = jnp.sum(jnp.transpose(weighted), axis=0, keepdims=True)
    ways = [(i, j) for i in range(zs) for j in range(xs) if i + j]
    for i, j in sorted(ways, key=lambda way: -min(way[0], zs - way[0]) - min(way[1], xs - way[1])):
        copy = pltpu.make_async_remote_copy(
            src_ref=score_all.at[seq_me],
            dst_ref=score_all.at[seq_me],
            send_sem=score_send.at[0],
            recv_sem=score_recv.at[0],
            device_id={"seq": lax.rem(z_me + i, zs) * xs + lax.rem(x_me + j, xs)},
            device_id_type=MESH,
        )
        copy.start()

    unit_z[z_me] = collect(unit_x, ux_recv, xs)
    share(unit_z, uz_send, uz_recv, z_me, zs, along_z)
    await_bytes(dots.at[pl.ds(0, tp - 1)], dot_send.at[0])
    sent(unit_x, ux_send, xs)

    unit_ref[...] = collect(unit_z, uz_recv, zs)
    sent(unit_z, uz_send, zs)
    score_ref[...] = collect(score_all, score_recv, xs * zs)
    sent(score_all, score_send, xs * zs)


def scale(factor, unit_ref, score_ref, unit_out, score_out):
    unit = unit_ref[...] * factor
    unit_out[0:2, :] = unit
    unit_out[2:3, :] = unit[1:2, :]
    score_out[...] = score_ref[...] * factor


def body(sizes, hidden, grad_out, router_w, norm_gain, gate_w, up_w, down_w, counts, order):
    xs, zs, ys, chunks, factor = sizes
    tp = ys * CORES
    tokens, width = hidden.shape
    features, units = gate_w.shape
    dma = pltpu.SemaphoreType.DMA
    f32, bf16 = jnp.float32, jnp.bfloat16
    in_hbm = pl.BlockSpec(memory_space=pl.ANY)
    in_vmem = pl.BlockSpec(memory_space=pltpu.VMEM)
    unit, score = pl.pallas_call(
        functools.partial(kernel, sizes),
        out_shape=(jax.ShapeDtypeStruct((2, units), f32), jax.ShapeDtypeStruct((1, width), f32)),
        in_specs=[
            in_hbm, in_hbm, in_hbm, in_hbm, in_hbm, in_hbm, in_hbm, in_hbm, in_hbm,
        ],
        out_specs=(in_vmem, in_vmem),
        scratch_shapes=[
            pltpu.VMEM((width, tokens), bf16),
            pltpu.VMEM((width, tokens), bf16),
            pltpu.VMEM((units, features), bf16),
            pltpu.VMEM((units, features), bf16),
            pltpu.VMEM((units, features), bf16),
            pltpu.VMEM((features,), f32),
            pltpu.VMEM((features,), bf16),
            pltpu.VMEM((1, order.shape[1]), jnp.int32),
            pltpu.SMEM((1,), jnp.int32),
            pltpu.VMEM((chunks, 2, tp, width, LANES), bf16),
            pltpu.VMEM((features, LANES), f32),
            pltpu.VMEM((features, LANES), f32),
            pltpu.VMEM((chunks, units, LANES), f32),
            pltpu.VMEM((chunks, units, LANES), f32),
            pltpu.VMEM((chunks, units, LANES), f32),
            pltpu.VMEM((2, units, LANES), f32),
            pltpu.VMEM((tp, chunks, LANES), f32),
            pltpu.VMEM((xs, 2, units), f32),
            pltpu.VMEM((zs, 2, units), f32),
            pltpu.VMEM((xs * zs, 1, width), f32),
            dma((9,)),
            pltpu.SemaphoreType.REGULAR((8,)),
            dma((chunks,)),
            dma((chunks, 2, tp)),
            dma((1,)),
            dma((1,)),
            dma((1,)),
            dma((1,)),
            dma((1,)),
            dma((1,)),
            dma((1,)),
            dma((1,)),
        ],
        compiler_params=pltpu.CompilerParams(
            collective_id=0, has_side_effects=True, vmem_limit_bytes=62 * 1024 * 1024
        ),
    )(
        hidden.T,
        grad_out.T,
        router_w,
        norm_gain,
        gate_w.T,
        up_w.T,
        down_w,
        counts,
        order,
    )
    unit, score = pl.pallas_call(
        functools.partial(scale, factor),
        out_shape=(jax.ShapeDtypeStruct((3, units), f32), jax.ShapeDtypeStruct((1, width), f32)),
        in_specs=[in_vmem, in_vmem],
        out_specs=(in_vmem, in_vmem),
    )(unit, score)
    return unit, score.reshape(width)


def solution(mesh):
    seq, tp = mesh.shape["seq"], mesh.shape["tp"]
    xs = X_CHIPS if seq % X_CHIPS == 0 else 1
    chunks = 3
    sizes = (xs, seq // xs, tp // CORES, chunks, float(LANES * seq) ** -0.5)
    in_specs = (
        P("seq", "tp"),
        P("seq", "tp"),
        P(),
        P(),
        P(None, "tp"),
        P(None, "tp"),
        P("tp", None),
        P("seq"),
        P("seq", None),
    )
    return jax.shard_map(
        functools.partial(body, sizes),
        mesh=mesh,
        in_specs=in_specs,
        out_specs=(P(None, "tp"), P("tp")),
        check_vma=False,
    )
```

```python
import functools

import jax
import jax.numpy as jnp
from jax import lax
from jax.experimental import pallas as pl
from jax.experimental.pallas import tpu as pltpu
from jax.sharding import PartitionSpec as P

MESH = pl.DeviceIdType.MESH
LANES = 128
CORES = 2
X_CHIPS = 4
EPSILON = 1e-06
ROOT = 0.7978845608028654
CUBIC = 0.044715


def column(row):
    return jnp.transpose(jnp.broadcast_to(row, (LANES, LANES)))


def kernel(
    sizes,
    hidden_hbm, grad_hbm, router_hbm, gain_hbm, gate_hbm, up_hbm, down_hbm, counts_hbm, order_hbm,
    unit_ref, score_ref,
    hidden_v, grad_v, gate_v, up_v, down_v, router_v, gain_v, order_v, count_v, held, gain_col, router_col,
    gate_sum, up_sum, back_sum, unit_sum, dots, unit_x, unit_z, score_all,
    load_sem, near_sem, ring_send, ring_recv, dot_send, dot_recv, ux_send, ux_recv, uz_send, uz_recv,
    score_send, score_recv,
):
    xs, zs, ys, chunks, factor = sizes
    tp = ys * CORES
    width = hidden_v.shape[0]
    tokens = hidden_v.shape[1]
    features = width * tp
    seq_me = lax.axis_index("seq")
    tp_me = lax.axis_index("tp")
    x_me, z_me = lax.rem(seq_me, xs), seq_me // xs
    y_me, core = tp_me // CORES, lax.rem(tp_me, CORES)
    sibling = y_me * CORES + (1 - core)

    def block_at(distance, of_core):
        return lax.rem(y_me + distance + ys, ys) * CORES + of_core

    right, left = block_at(1, core), block_at(-1, core)

    loads = [
        pltpu.make_async_copy(source, target, load_sem.at[i])
        for i, (source, target) in enumerate(
            [
                (order_hbm, order_v), (counts_hbm, count_v), (hidden_hbm, hidden_v), (grad_hbm, grad_v),
                (router_hbm, router_v), (gain_hbm, gain_v), (gate_hbm, gate_v), (up_hbm, up_v), (down_hbm, down_v),
            ]
        )
    ]
    for load in loads[:4]:
        load.start()

    barrier = pltpu.get_barrier_semaphore()
    along_x = lambda i: z_me * xs + lax.rem(i + xs, xs)
    along_z = lambda i: lax.rem(i + zs, zs) * xs + x_me
    beside_x = [along_x(x_me + i) for i in ((1, -1) if xs > 2 else (1,) if xs > 1 else ())]
    beside_z = [along_z(z_me + i) for i in ((1, -1) if zs > 2 else (1,) if zs > 1 else ())]
    beside_y = [right, left] if ys > 2 else [right]
    for peer in beside_y + [sibling]:
        pl.semaphore_signal(barrier, inc=1, device_id={"tp": peer}, device_id_type=MESH)
    for peer in beside_x + beside_z:
        pl.semaphore_signal(barrier, inc=1, device_id={"seq": peer}, device_id_type=MESH)

    rounds = zs // 2 + xs // 2 - 1
    relayed = []

    def relay():
        i = len(relayed)
        if i > rounds:
            return
        relayed.append(i)
        if i > 0:
            pl.semaphore_wait(near_sem.at[i - 1], len(beside_x + beside_z))
        if i < rounds:
            for peer in beside_x + beside_z:
                pl.semaphore_signal(near_sem.at[i], inc=1, device_id={"seq": peer}, device_id_type=MESH)

    token = lax.broadcasted_iota(jnp.int32, (tokens, LANES), 0)
    slot = lax.broadcasted_iota(jnp.int32, (1, LANES), 1)
    loads[0].wait()
    loads[1].wait()
    count = count_v[0]

    def choose(chunk):
        wanted = order_v[:, chunk * LANES : (chunk + 1) * LANES]
        wanted = jnp.where(slot + chunk * LANES < count, wanted, -1)
        return jnp.where(token == wanted, 1.0, 0.0).astype(jnp.bfloat16)

    def pick(chunk, array, chosen):
        rows = jnp.dot((hidden_v, grad_v)[array][...], chosen, preferred_element_type=jnp.float32)
        held[chunk, array, tp_me] = rows.astype(jnp.bfloat16)

    ring_sent = [0] * chunks

    def pass_on(chunk, array, block, way):
        target = (right, left, sibling)[way]
        copy = pltpu.make_async_remote_copy(
            src_ref=held.at[chunk, array, block],
            dst_ref=held.at[chunk, array, block],
            send_sem=ring_send.at[chunk],
            recv_sem=ring_recv.at[chunk, array, block],
            device_id={"tp": target},
            device_id_type=MESH,
        )
        copy.start()
        ring_sent[chunk] += 1

    def await_bytes(view, semaphore):
        pltpu.make_async_copy(view, view, semaphore).wait()

    def arrive(chunk, array, block):
        pltpu.make_async_copy(
            held.at[chunk, array, block], held.at[chunk, array, block], ring_recv.at[chunk, array, block]
        ).wait()

    half = ys // 2

    def open_ring(chunk):
        chosen = choose(chunk)
        for array in range(2):
            if chunk == 0:
                loads[2 + array].wait()
            pick(chunk, array, chosen)
            if chunk == 0 and array == 0:
                pl.semaphore_wait(barrier, len(beside_y) + 1 + len(beside_x) + len(beside_z))
            for way in range(2):
                if half > 1 or way == array:
                    pass_on(chunk, array, tp_me, way)

    def ring_step(chunk, distance):
        last = distance == half
        across = []
        for array in range(2):
            for way in range(2):
                if last and array != way:
                    continue
                block = block_at(-distance if way == 0 else distance, core)
                arrive(chunk, array, block)
                if distance + 1 < half or (distance + 1 == half and array == way):
                    pass_on(chunk, array, block, way)
                across.append((array, block))
        for array, block in across:
            pass_on(chunk, array, block, 2)

    def sibling_step(chunk, distance):
        for array in range(2):
            for way in range(2):
                if distance == 0 and way == 1 or distance == half and way != array:
                    continue
                arrive(chunk, array, block_at(-distance if way == 0 else distance, 1 - core))

    groups = ys // 2
    first = y_me // 2
    lean = 2 * lax.rem(y_me, 2) - 1
    group_order = [first] if groups == 1 else [first, first + lean, first - lean, first + 2]
    group_after = [1, 2, 3, 4]
    if groups == 2:
        group_order, group_after = [first, first + 1], [1, 2]
    if groups == 1:
        group_after = [1]
    depth = features // groups

    def multiply(picked, place):
        group = lax.rem(group_order[place] + groups, groups)
        at = pl.ds(pl.multiple_of(group * depth, LANES), depth)
        pieces = pl.ds(group * (tp // groups), tp // groups)
        scaled, cotangent, sums = [], [], []
        for chunk in picked:
            values = held[chunk, 0, pieces].reshape(depth, LANES).astype(jnp.float32)
            scaled.append((values * gain_col[at, :]).astype(jnp.bfloat16))
            cotangent.append(held[chunk, 1, pieces].reshape(depth, LANES))
            squares = jnp.sum(values * values, axis=0, keepdims=True)
            logit = jnp.sum(values * router_col[at, :], axis=0, keepdims=True)
            sums.append((squares, logit))
        scaled = jnp.concatenate(scaled, axis=1)
        cotangent = jnp.concatenate(cotangent, axis=1)
        for total, weight, rows in ((gate_sum, gate_v, scaled), (up_sum, up_v, scaled), (back_sum, down_v, cotangent)):
            product = jnp.dot(weight[:, at], rows, preferred_element_type=jnp.float32)
            for i, chunk in enumerate(picked):
                part = product[:, i * LANES : (i + 1) * LANES]
                if place == 0:
                    total[chunk] = part
                else:
                    total[chunk] += part
        return sums

    def far_first(count_of, gap):
        return sorted(range(1, count_of), key=lambda step: -min(step // gap, (count_of - step) // gap))

    def share_dots():
        for step in far_first(tp, CORES):
            copy = pltpu.make_async_remote_copy(
                src_ref=dots.at[tp_me],
                dst_ref=dots.at[tp_me],
                send_sem=dot_send.at[0],
                recv_sem=dot_recv.at[0],
                device_id={"tp": lax.rem(tp_me + step, tp)},
                device_id_type=MESH,
            )
            copy.start()

    def finish(chunk, squares, logit):
        inverse = lax.rsqrt(squares / features + EPSILON)
        prob = 1.0 / (1.0 + jnp.exp(-logit))
        gate = gate_sum[chunk] * inverse
        up = up_sum[chunk] * inverse
        back = back_sum[chunk]
        square = gate * gate
        bend = jnp.tanh(ROOT * gate * (1.0 + CUBIC * square))
        plus = 0.5 * (1.0 + bend)
        slope = plus + 0.5 * gate * (1.0 - bend * bend) * (ROOT * (1.0 + (3.0 * CUBIC) * square))
        act = gate * plus
        h_back = act * up * back
        dots[tp_me, chunk : chunk + 1, :] = jnp.sum(h_back, axis=0, keepdims=True)
        term = gate * up * slope * back * prob
        if chunk == 0:
            unit_sum[0] = term
            unit_sum[1] = h_back * prob
        else:
            unit_sum[0] += term
            unit_sum[1] += h_back * prob
        return prob

    for chunk in range(chunks):
        open_ring(chunk)
        if chunk == 0:
            relay()
            for load in loads[4:]:
                load.start()
    relay()
    for chunk in range(chunks):
        for array in range(2):
            pass_on(chunk, array, tp_me, 2)
    loads[4].wait()
    loads[5].wait()
    gain = gain_v[...].astype(jnp.float32)
    for i in range(features // LANES):
        at = slice(i * LANES, (i + 1) * LANES)
        gain_col[at, :] = column(gain[at].reshape(1, LANES))
        router_col[at, :] = column(router_v[at].reshape(1, LANES))
    for load in loads[6:]:
        load.wait()

    probs = [None] * chunks
    totals = [None] * chunks

    def compute(picked, place):
        for chunk in picked:
            sibling_step(chunk, group_after[place])
        sums = multiply(picked, place)
        for chunk, more in zip(picked, sums):
            totals[chunk] = more if place == 0 else (totals[chunk][0] + more[0], totals[chunk][1] + more[1])
        if place == len(group_after) - 1:
            for chunk in picked:
                probs[chunk] = finish(chunk, *totals[chunk])

    for chunk in range(chunks):
        sibling_step(chunk, 0)
    waiting = []
    for distance in range(1, half + 1):
        for chunk in range(chunks):
            ring_step(chunk, distance)
            if waiting and not (distance == half and chunk == chunks - 1):
                compute(*waiting.pop(0))
            if distance in group_after:
                waiting.append(([chunk], group_after.index(distance)))
            relay()
    if waiting:
        compute([chunk for picked, _ in waiting for chunk in picked], waiting[0][1])
    share_dots()

    def share(buffer, send, recv, mine, count_of, peer_of):
        for step in far_first(count_of, 1):
            copy = pltpu.make_async_remote_copy(
                src_ref=buffer.at[mine],
                dst_ref=buffer.at[mine],
                send_sem=send.at[0],
                recv_sem=recv.at[0],
                device_id={"seq": peer_of(lax.rem(mine + step, count_of))},
                device_id_type=MESH,
            )
            copy.start()

    def sent(buffer, send, count_of):
        if count_of > 1:
            await_bytes(buffer.at[pl.ds(0, count_of - 1)], send.at[0])

    def collect(buffer, recv, count_of):
        if count_of > 1:
            await_bytes(buffer.at[pl.ds(0, count_of - 1)], recv.at[0])
        total = buffer[0]
        for i in range(1, count_of):
            total = total + buffer[i]
        return total

    while len(relayed) <= rounds:
        relay()

    for i in range(2):
        unit_x[x_me, i : i + 1, :] = jnp.sum(jnp.transpose(unit_sum[i]), axis=0, keepdims=True)
    share(unit_x, ux_send, ux_recv, x_me, xs, along_x)
    for chunk in range(chunks):
        assert ring_sent[chunk] == 2 * (tp - 1)
        await_bytes(held.at[chunk, :, pl.ds(0, tp - 1)], ring_send.at[chunk])

    share_of_router = router_col[pl.ds(pl.multiple_of(tp_me * width, 8), width), :]
    terms = [
        held[chunk, 0, tp_me].astype(jnp.float32) * share_of_router * (probs[chunk] * (1.0 - probs[chunk]))
        for chunk in range(chunks)
    ]
    await_bytes(dots.at[pl.ds(0, tp - 1)], dot_recv.at[0])
    total = dots[0]
    for i in range(1, tp):
        total = total + dots[i]
    weighted = terms[0] * total[0:1, :]
    for chunk in range(1, chunks):
        weighted = weighted + terms[chunk] * total[chunk : chunk + 1, :]
    score_all[seq_me] = jnp.sum(jnp.transpose(weighted), axis=0, keepdims=True)
    ways = [(i, j) for i in range(zs) for j in range(xs) if i + j]
    for i, j in sorted(ways, key=lambda way: -min(way[0], zs - way[0]) - min(way[1], xs - way[1])):
        copy = pltpu.make_async_remote_copy(
            src_ref=score_all.at[seq_me],
            dst_ref=score_all.at[seq_me],
            send_sem=score_send.at[0],
            recv_sem=score_recv.at[0],
            device_id={"seq": lax.rem(z_me + i, zs) * xs + lax.rem(x_me + j, xs)},
            device_id_type=MESH,
        )
        copy.start()

    unit_z[z_me] = collect(unit_x, ux_recv, xs)
    share(unit_z, uz_send, uz_recv, z_me, zs, along_z)
    await_bytes(dots.at[pl.ds(0, tp - 1)], dot_send.at[0])
    sent(unit_x, ux_send, xs)

    unit_ref[...] = collect(unit_z, uz_recv, zs)
    sent(unit_z, uz_send, zs)
    score_ref[...] = collect(score_all, score_recv, xs * zs)
    sent(score_all, score_send, xs * zs)


def scale(factor, unit_ref, score_ref, unit_out, score_out):
    unit = unit_ref[...] * factor
    unit_out[0:2, :] = unit
    unit_out[2:3, :] = unit[1:2, :]
    score_out[...] = score_ref[...] * factor


def body(sizes, hidden, grad_out, router_w, norm_gain, gate_w, up_w, down_w, counts, order):
    xs, zs, ys, chunks, factor = sizes
    tp = ys * CORES
    tokens, width = hidden.shape
    features, units = gate_w.shape
    dma = pltpu.SemaphoreType.DMA
    f32, bf16 = jnp.float32, jnp.bfloat16
    in_hbm = pl.BlockSpec(memory_space=pl.ANY)
    in_vmem = pl.BlockSpec(memory_space=pltpu.VMEM)
    unit, score = pl.pallas_call(
        functools.partial(kernel, sizes),
        out_shape=(jax.ShapeDtypeStruct((2, units), f32), jax.ShapeDtypeStruct((1, width), f32)),
        in_specs=[
            in_hbm, in_hbm, in_hbm, in_hbm, in_hbm, in_hbm, in_hbm, in_hbm, in_hbm,
        ],
        out_specs=(in_vmem, in_vmem),
        scratch_shapes=[
            pltpu.VMEM((width, tokens), bf16),
            pltpu.VMEM((width, tokens), bf16),
            pltpu.VMEM((units, features), bf16),
            pltpu.VMEM((units, features), bf16),
            pltpu.VMEM((units, features), bf16),
            pltpu.VMEM((features,), f32),
            pltpu.VMEM((features,), bf16),
            pltpu.VMEM((1, order.shape[1]), jnp.int32),
            pltpu.SMEM((1,), jnp.int32),
            pltpu.VMEM((chunks, 2, tp, width, LANES), bf16),
            pltpu.VMEM((features, LANES), f32),
            pltpu.VMEM((features, LANES), f32),
            pltpu.VMEM((chunks, units, LANES), f32),
            pltpu.VMEM((chunks, units, LANES), f32),
            pltpu.VMEM((chunks, units, LANES), f32),
            pltpu.VMEM((2, units, LANES), f32),
            pltpu.VMEM((tp, chunks, LANES), f32),
            pltpu.VMEM((xs, 2, units), f32),
            pltpu.VMEM((zs, 2, units), f32),
            pltpu.VMEM((xs * zs, 1, width), f32),
            dma((9,)),
            pltpu.SemaphoreType.REGULAR((8,)),
            dma((chunks,)),
            dma((chunks, 2, tp)),
            dma((1,)),
            dma((1,)),
            dma((1,)),
            dma((1,)),
            dma((1,)),
            dma((1,)),
            dma((1,)),
            dma((1,)),
        ],
        compiler_params=pltpu.CompilerParams(
            collective_id=0, has_side_effects=True, vmem_limit_bytes=62 * 1024 * 1024
        ),
    )(
        hidden.T,
        grad_out.T,
        router_w,
        norm_gain,
        gate_w.T,
        up_w.T,
        down_w,
        counts,
        order,
    )
    unit, score = pl.pallas_call(
        functools.partial(scale, factor),
        out_shape=(jax.ShapeDtypeStruct((3, units), f32), jax.ShapeDtypeStruct((1, width), f32)),
        in_specs=[in_vmem, in_vmem],
        out_specs=(in_vmem, in_vmem),
        compiler_params=pltpu.CompilerParams(vmem_limit_bytes=62 * 1024 * 1024),
    )(unit, score)
    return unit, score.reshape(width)


def solution(mesh):
    seq, tp = mesh.shape["seq"], mesh.shape["tp"]
    xs = X_CHIPS if seq % X_CHIPS == 0 else 1
    chunks = 3
    sizes = (xs, seq // xs, tp // CORES, chunks, float(LANES * seq) ** -0.5)
    in_specs = (
        P("seq", "tp"),
        P("seq", "tp"),
        P(),
        P(),
        P(None, "tp"),
        P(None, "tp"),
        P("tp", None),
        P("seq"),
        P("seq", None),
    )
    return jax.shard_map(
        functools.partial(body, sizes),
        mesh=mesh,
        in_specs=in_specs,
        out_specs=(P(None, "tp"), P("tp")),
        check_vma=False,
    )
```
